32 devices in a mesh: row: 8 (over y, x, core), col: 4 (over z).
Axes of the slice: x: 2, y: 2, z: 4, core: 2. Of those that a mesh axis runs over, the one named last changes fastest.
Arguments:
- query_in: bfloat16 [2048, 8192], P('row', 'col'), may hold values from -6 to 6
- key_in: bfloat16 [2048, 8192], P('row', 'col'), may hold values from -6 to 6
- value_in: bfloat16 [2048, 8192], P('row', 'col'), may hold values from -6 to 6
- filters: float32 [512, 128], P('col'), may hold values from -0.5 to 0.5
- out_weight: bfloat16 [8192, 8192], P('row', 'col'), may hold values from -0.0625 to 0.0625
- out_grad: bfloat16 [2048, 8192], P('row', 'col'), may hold values from -6 to 6
Outputs:
- mixed: bfloat16 [2048, 8192], P('row', 'col')
- query_grad: bfloat16 [2048, 8192], P('row', 'col')
- key_grad: bfloat16 [2048, 8192], P('row', 'col')
- value_grad: bfloat16 [2048, 8192], P('row', 'col')
- weight_grad: bfloat16 [8192, 8192], P('row', 'col')
- filter_grad: float32 [512, 128], P('col')
The draws below stay inside these ranges and needn't reach their ends.
All inputs are finite; a program needn't handle non-finite values.
Results may differ from the reference program's by a relative error of at most 0.018.
Values may be sent and summed in bfloat16 or wider, within the bound.
No kernel may reach another device: no remote copies, remote signals or barrier semaphores. Data moves between devices by JAX's collectives and lax.ppermute only.
A program may use at most 192 MiB of HBM per device.

```python
import math
import jax
import jax.numpy as jnp
from jax import lax

D = 8192
FILT = 128
GROUP = 16
TOK_DEV = 256
TOKENS = 2048
G = 512
N_ROW = 8
N_COL = 4


def level_of(stream_key, shape, cuts, low, largest):
    def one(dim, shards_of):
        draws = jax.random.uniform(jax.random.fold_in(jax.random.fold_in(stream_key, 6), dim), (shards_of,), jnp.float32, low / len(cuts), largest / len(cuts))
        return jnp.repeat(jnp.exp(draws), shape[dim] // shards_of).reshape((-1,) + (1,) * (len(shape) - dim - 1))

    gain = one(*cuts[0])
    for cut in cuts[1:]:
        gain = gain * one(*cut)
    return gain


def bell_draw(key, dims, spread, bound, pieces=(), kind=jnp.bfloat16):
    gain = level_of(key, dims, pieces, -0.22, 0.18) if pieces else 1.0
    drawn = jax.random.normal(key, dims, jnp.float32) * spread * gain
    return jnp.minimum(jnp.maximum(drawn, -bound), bound).astype(kind)


def setup_inputs(seed: int = 0) -> dict:
    keys = jax.random.split(jax.random.key(seed), 7)
    return {
        "query_in": bell_draw(keys[0], (TOKENS, D), 1.0, 6.0, ((0, 8), (1, 4))),
        "key_in": bell_draw(keys[1], (TOKENS, D), 1.0, 6.0, ((0, 8), (1, 4))),
        "value_in": bell_draw(keys[2], (TOKENS, D), 1.0, 6.0, ((0, 8), (1, 4))),
        "filters": bell_draw(keys[3], (G, FILT), FILT ** -0.5, 0.5, ((0, 4),), jnp.float32),
        "out_weight": bell_draw(keys[4], (D, D), D ** -0.5, 0.0625, ((0, 8), (1, 4))),
        "out_grad": bell_draw(keys[5], (TOKENS, D), 1.0, 6.0, ((0, 8), (1, 4))),
    }


def reference(query_in, key_in, value_in, filters, out_weight, out_grad):
    f32 = jnp.float32
    bf16 = jnp.bfloat16
    query32 = query_in.astype(f32)
    key32 = key_in.astype(f32)
    value32 = value_in.astype(f32)
    product = key32 * value32
    taps = jnp.repeat(filters.astype(f32), GROUP, axis=0)
    ahead = jnp.concatenate([jnp.zeros((FILT, D), f32), product], 0)

    def conv_step(m, acc):
        part = lax.dynamic_slice_in_dim(ahead, FILT - m, TOKENS, 0)
        return acc + part * lax.dynamic_index_in_dim(taps, m, 1, False)
    conv = lax.fori_loop(0, FILT, conv_step, jnp.zeros((TOKENS, D), f32))
    gated = (query32 * conv).astype(bf16)
    mixed = jnp.dot(gated, out_weight, preferred_element_type=f32).astype(bf16)
    width = D // N_COL

    def grad_step(acc, index):
        start = (index * width).astype(jnp.int32)
        cols = lax.dynamic_slice_in_dim(out_grad, start, width, 1)
        rows = lax.dynamic_slice_in_dim(out_weight, start, width, 1)
        term = lax.dot_general(cols, rows, (((1,), (1,)), ((), ())), preferred_element_type=f32)
        term = lax.optimization_barrier(term.astype(bf16)).astype(f32)
        return (acc + term, None)
    grad_gated, _ = lax.scan(grad_step, jnp.zeros((TOKENS, D), f32), jnp.arange(N_COL, dtype=jnp.int32))
    query_grad = (grad_gated * conv).astype(bf16)
    grad_conv = grad_gated * query32
    behind = jnp.concatenate([grad_conv, jnp.zeros((FILT, D), f32)], 0)

    def back_step(m, acc):
        part = lax.dynamic_slice_in_dim(behind, m, TOKENS, 0)
        return acc + part * lax.dynamic_index_in_dim(taps, m, 1, False)
    grad_product = lax.fori_loop(0, FILT, back_step, jnp.zeros((TOKENS, D), f32))
    key_grad = (grad_product * value32).astype(bf16)
    value_grad = (grad_product * key32).astype(bf16)

    def filter_tap(m):
        part = lax.dynamic_slice_in_dim(ahead, FILT - m, TOKENS, 0)
        return lax.optimization_barrier(jnp.sum((grad_conv * part).reshape(TOKENS, D // GROUP, GROUP), axis=(0, 2)))
    per_tap = lax.map(filter_tap, jnp.arange(FILT, dtype=jnp.int32))
    filter_grad = per_tap.T * (1.0 / math.sqrt(TOKENS * GROUP))

    def weight_step(acc, index):
        start = (index * TOK_DEV).astype(jnp.int32)
        rows_a = lax.dynamic_slice_in_dim(gated, start, TOK_DEV, 0)
        rows_b = lax.dynamic_slice_in_dim(out_grad, start, TOK_DEV, 0)
        term = lax.dot_general(rows_a, rows_b, (((0,), (0,)), ((), ())), preferred_element_type=f32)
        term = lax.optimization_barrier(term.astype(bf16)).astype(f32)
        return (acc + term, None)
    weight_sum, _ = lax.scan(weight_step, jnp.zeros((D, D), f32), jnp.arange(N_ROW, dtype=jnp.int32))
    weight_grad = (weight_sum * (1.0 / math.sqrt(TOKENS))).astype(bf16)
    return (mixed, query_grad, key_grad, value_grad, weight_grad, filter_grad)
```

```python
import functools
import math

import jax
import jax.numpy as jnp
from jax import lax
from jax.experimental import pallas as pl
from jax.experimental.pallas import tpu as pltpu
from jax.sharding import PartitionSpec as P

LANES = 128
STEP = 512
f32 = jnp.float32
bf16 = jnp.bfloat16


def band(base, index, span):
    row = jnp.broadcast_to(base[index : index + 1], (span, 2 * span))
    return pltpu.roll(row, 0, 1, stride=1, stride_axis=0).astype(bf16)


def banded(base, column, first, owner, span, group):
    total = jnp.zeros(owner.shape, f32)
    for g in range(LANES // group):
        value = jnp.dot(band(base, first + g, span), column, preferred_element_type=f32)
        total = jnp.where(owner == g, value, total)
    return total


def conv_kernel(span, group, turn_ref, base_ref, before_ref, here_ref, query_ref, gated_ref, conv_ref):
    window = jnp.concatenate([before_ref[...], here_ref[...]], 0)
    owner = lax.broadcasted_iota(jnp.int32, (span, LANES), 1) // group
    for start in range(0, window.shape[1], LANES):
        cut = slice(start, start + LANES)
        conv = banded(base_ref[...], window[:, cut], start // group, owner, span, group)
        conv_ref[:, cut] = conv
        gated_ref[:, cut] = (query_ref[:, cut].astype(f32) * conv).astype(bf16)


def conv_call(turn, base, before, before_at, here, at, query, span, group):
    width = here.shape[1]
    lanes = min(width, STEP)

    def block(row):
        return pl.BlockSpec((span, lanes), lambda i, turn: (row, i))

    return pl.pallas_call(
        functools.partial(conv_kernel, span, group),
        grid_spec=pltpu.PrefetchScalarGridSpec(
            num_scalar_prefetch=1,
            grid=(width // lanes,),
            in_specs=[
                pl.BlockSpec((lanes // group, 2 * span), lambda i, turn: (i, 0)),
                block(before_at),
                block(at),
                block(at),
            ],
            out_specs=[
                pl.BlockSpec((span, lanes), lambda i, turn: (0, i ^ turn[0])),
                block(0),
            ],
        ),
        out_shape=[
            jax.ShapeDtypeStruct((span, width), bf16),
            jax.ShapeDtypeStruct((span, width), f32),
        ],
        cost_estimate=pl.CostEstimate(
            flops=4 * span * span * width * LANES // group,
            bytes_accessed=12 * span * width,
            transcendentals=0,
        ),
        name="conv",
    )(turn, base, before, here, query)


def taps_kernel(span, group, turn_ref, grad_ref, low_ref, high_ref, query_ref, rim_ref, product_ref, query_grad_ref, grad_conv_ref, taps_ref):
    rows = lax.broadcasted_iota(jnp.int32, (span, span), 0)
    columns = lax.broadcasted_iota(jnp.int32, (span, span), 1)
    flip = jnp.where(rows + columns == span - 1, 1.0, 0.0).astype(bf16)
    owner = lax.broadcasted_iota(jnp.int32, (span, 2 * LANES), 1) % LANES // group
    for start in range(0, query_ref.shape[1], LANES):
        cut = slice(start, start + LANES)
        grad = grad_ref[0, :, cut].astype(f32)
        conv = jnp.concatenate([low_ref[:, cut], high_ref[:, cut]], 0)
        query_grad_ref[:, cut] = (grad * conv).astype(bf16)
        grad_conv = (grad * query_ref[:, cut].astype(f32)).astype(bf16)
        grad_conv_ref[:, cut] = grad_conv
        left = jnp.concatenate([grad_conv[:span], grad_conv[span:]], 1)
        left = jnp.dot(flip, left, preferred_element_type=f32).astype(bf16)
        late = product_ref[:, cut]
        early = jnp.concatenate([rim_ref[:, cut], late[:span]], 0)
        right = jnp.concatenate([early, late], 1)
        for g in range(LANES // group):
            one = jnp.where(owner == g, left, jnp.zeros_like(left))
            corr = lax.dot_general(one, right, (((1,), (1,)), ((), ())), preferred_element_type=f32)
            lined = pltpu.roll(corr, 0, 1, stride=1, stride_axis=0)
            at = start // group + g
            taps_ref[at : at + 1] = jnp.sum(lined[:, span:], axis=0, keepdims=True)


def taps_call(turn, grad, low, high, query, rim, product, span, group):
    tokens, width = query.shape
    lanes = grad.shape[2]

    def block(rows):
        return pl.BlockSpec((rows, lanes), lambda i, turn: (0, i))

    return pl.pallas_call(
        functools.partial(taps_kernel, span, group),
        grid_spec=pltpu.PrefetchScalarGridSpec(
            num_scalar_prefetch=1,
            grid=(width // lanes,),
            in_specs=[
                pl.BlockSpec((1, tokens, lanes), lambda i, turn: (i ^ turn[0], 0, 0)),
                block(span),
                block(span),
                block(tokens),
                block(span),
                block(tokens),
            ],
            out_specs=[
                block(tokens),
                block(tokens),
                pl.BlockSpec((lanes // group, span), lambda i, turn: (i, 0)),
            ],
        ),
        out_shape=[
            jax.ShapeDtypeStruct((tokens, width), bf16),
            jax.ShapeDtypeStruct((tokens, width), bf16),
            jax.ShapeDtypeStruct((width // group, span), f32),
        ],
        cost_estimate=pl.CostEstimate(
            flops=8 * span * tokens * width * LANES // group,
            bytes_accessed=16 * tokens * width,
            transcendentals=0,
        ),
        name="taps",
    )(turn, grad, low, high, query, rim, product)


def back_kernel(span, group, base_ref, grad_conv_ref, rim_ref, key_ref, value_ref, key_grad_ref, value_grad_ref):
    owner = lax.broadcasted_iota(jnp.int32, (span, 2 * LANES), 1) % LANES // group
    for start in range(0, key_ref.shape[1], LANES):
        cut = slice(start, start + LANES)
        here = grad_conv_ref[:, cut]
        after = jnp.concatenate([here[span:], rim_ref[:, cut]], 0)
        column = jnp.concatenate([here, after], 1)
        total = banded(base_ref[...], column, start // group, owner, span, group)
        product = jnp.concatenate([total[:, :LANES], total[:, LANES:]], 0)
        key_grad_ref[:, cut] = (product * value_ref[:, cut].astype(f32)).astype(bf16)
        value_grad_ref[:, cut] = (product * key_ref[:, cut].astype(f32)).astype(bf16)


def back_call(base, grad_conv, rim, key, value, span, group):
    tokens, width = key.shape
    lanes = min(width, STEP)

    def block(rows):
        return pl.BlockSpec((rows, lanes), lambda i: (0, i))

    return pl.pallas_call(
        functools.partial(back_kernel, span, group),
        grid=(width // lanes,),
        in_specs=[
            pl.BlockSpec((lanes // group, 2 * span), lambda i: (i, 0)),
            block(tokens),
            block(span),
            block(tokens),
            block(tokens),
        ],
        out_specs=[block(tokens), block(tokens)],
        out_shape=[
            jax.ShapeDtypeStruct((tokens, width), bf16),
            jax.ShapeDtypeStruct((tokens, width), bf16),
        ],
        cost_estimate=pl.CostEstimate(
            flops=4 * span * tokens * width * LANES // group,
            bytes_accessed=12 * tokens * width,
            transcendentals=0,
        ),
        name="back",
    )(base, grad_conv, rim, key, value)


def from_behind(shard, by):
    size = lax.axis_size("row")
    pairs = [(i, i + by) for i in range(size) if 0 <= i + by < size]
    return lax.ppermute(shard, "row", pairs)


def exchange(shard, bits):
    size = lax.axis_size("row")
    return lax.ppermute(shard, "row", [(i, i ^ bits) for i in range(size)])


def ring(shard):
    size = lax.axis_size("col")
    return lax.ppermute(shard, "col", [(i, (i + 1) % size) for i in range(size)])


def dot_nt(a, b):
    return lax.dot_general(a, b, (((1,), (1,)), ((), ())), preferred_element_type=f32)


def dot_tn(a, b):
    return lax.dot_general(a, b, (((0,), (0,)), ((), ())), preferred_element_type=f32)


def projection(gated, out_weight, out_grad, total_tokens):
    cols = lax.axis_size("col")
    core = lax.axis_index("row") % 2
    chip = lax.axis_index("row") // 2
    plane = lax.axis_index("col")
    span, width = gated[0].shape
    blocks = len(gated)
    half = out_weight.shape[0]
    lanes = width // cols
    pair = jnp.concatenate([out_weight, exchange(out_weight, 1)], 0)

    sent = [out_grad] + [exchange(out_grad, 2 * d) for d in range(1, cols)]
    grads = jnp.concatenate([g[h * span : (h + 1) * span] for h in range(blocks) for g in sent], 0)

    total = None
    for step in range(cols):
        part = (plane + 2 * cols - 1 - step) % cols
        rows = lax.dynamic_slice_in_dim(pair, part * lanes, lanes, 0)
        value = dot_nt(grads, rows)
        if total is not None:
            value = value + ring(total).astype(f32)
        total = value.astype(bf16)
    summed = total.reshape(blocks, cols, span, lanes)
    grad_gated = []
    for e in range(cols):
        piece = lax.dynamic_index_in_dim(summed, chip ^ plane ^ e, 1, False)
        pairs = [
            ((2 * q + s) * cols + j, (2 * (j ^ e) + s) * cols + q)
            for q in range(cols)
            for s in range(2)
            for j in range(cols)
        ]
        grad_gated.append(lax.ppermute(piece.reshape(blocks * span, lanes), ("row", "col"), pairs))
    grad_gated = jnp.stack(grad_gated)

    held = [None] * blocks
    mixed = [None] * blocks
    for h in reversed(range(blocks)):
        pieces = [gated[h]]
        for _ in range(1, cols):
            pieces.append(ring(pieces[-1]))
        stack = jnp.stack(pieces)
        own = lax.dynamic_index_in_dim(stack, (plane - chip) % cols, 0, False)
        came = []
        for d in range(1, cols):
            piece = lax.dynamic_index_in_dim(stack, (plane - (chip ^ d)) % cols, 0, False)
            came.append(exchange(piece, 2 * d))
        held[h] = [own] + came
        partial = jnp.dot(jnp.concatenate(came, 0), pair, preferred_element_type=f32).astype(bf16)
        value = jnp.dot(own, pair, preferred_element_type=f32)
        for d in range(1, cols):
            value = value + exchange(partial[(d - 1) * span : d * span], 2 * d).astype(f32)
        mixed[h] = value.astype(bf16)
    mixed = jnp.concatenate(mixed, 0)

    tokens = jnp.concatenate([piece for h in held for piece in h], 0)
    other = exchange(dot_tn(tokens[:, half:], grads).astype(bf16), 1)
    weight_sum = dot_tn(tokens[:, :half], grads) + other.astype(f32)
    weight_grad = (weight_sum * (1.0 / math.sqrt(total_tokens))).astype(bf16)
    return mixed, grad_gated, weight_grad


def projection_gathered(gated, out_weight, out_grad, total_tokens):
    panel = lax.all_gather(jnp.concatenate(gated, 0), "col", axis=1, tiled=True)
    weights = lax.all_gather(out_weight, "row", axis=0, tiled=True)
    mixed = jnp.dot(panel, weights, preferred_element_type=f32).astype(bf16)
    partial = dot_nt(out_grad, weights).astype(bf16)
    grad_gated = lax.psum_scatter(partial, "col", scatter_dimension=1, tiled=True)
    tokens, width = grad_gated.shape
    lanes = min(width, STEP)
    grad_gated = grad_gated.reshape(tokens, width // lanes, lanes).transpose(1, 0, 2)
    weight_sum = lax.psum_scatter(
        dot_tn(panel, out_grad).astype(bf16), "row", scatter_dimension=0, tiled=True
    ).astype(f32)
    weight_grad = (weight_sum * (1.0 / math.sqrt(total_tokens))).astype(bf16)
    return mixed, grad_gated, weight_grad


def shards(query_in, key_in, value_in, filters, out_weight, out_grad):
    tokens, width = query_in.shape
    groups, span = filters.shape
    group = width // groups
    rows, cols = lax.axis_size("row"), lax.axis_size("col")
    total_tokens = tokens * rows
    even = cols & (cols - 1) == 0
    paired = even and rows == 2 * cols and width == 2 * out_weight.shape[0] and width == cols * STEP
    core = lax.axis_index("row") % 2
    chip = lax.axis_index("row") // 2
    turn_gated = core * (cols // 2) if paired else core * 0
    turn_grad = turn_gated ^ chip if paired else core * 0

    product = (key_in.astype(f32) * value_in.astype(f32)).astype(bf16)
    rim = from_behind(product[-span:], 1)
    zeros = jnp.zeros((groups, span - 1), f32)
    causal = jnp.concatenate([zeros[:, :1], filters[:, ::-1], zeros], 1)
    anticausal = jnp.concatenate([filters, zeros, zeros[:, :1]], 1)
    turn = turn_gated.astype(jnp.int32).reshape(1)
    gated_high, conv_high = conv_call(turn, causal, product, 0, product, 1, query_in, span, group)
    gated_low, conv_low = conv_call(turn, causal, rim, 0, product, 0, query_in, span, group)

    project = projection if paired else projection_gathered
    mixed, grad_gated, weight_grad = project([gated_low, gated_high], out_weight, out_grad, total_tokens)

    turn = turn_grad.astype(jnp.int32).reshape(1)
    query_grad, grad_conv, taps = taps_call(turn, grad_gated, conv_low, conv_high, query_in, rim, product, span, group)
    grad_rim = from_behind(grad_conv[:span], -1)
    key_grad, value_grad = back_call(anticausal, grad_conv, grad_rim, key_in, value_in, span, group)
    bits = 1
    while bits < rows:
        taps = taps + exchange(taps, bits)
        bits *= 2
    filter_grad = taps[:, ::-1] * (1.0 / math.sqrt(total_tokens * group))
    return (mixed, query_grad, key_grad, value_grad, weight_grad, filter_grad)


def solution(mesh):
    placed = (
        P("row", "col"),
        P("row", "col"),
        P("row", "col"),
        P("col", None),
        P("row", "col"),
        P("row", "col"),
    )
    return jax.shard_map(
        shards,
        mesh=mesh,
        in_specs=placed,
        out_specs=(
            P("row", "col"),
            P("row", "col"),
            P("row", "col"),
            P("row", "col"),
            P("row", "col"),
            P("col", None),
        ),
        check_vma=False,
    )
```

```python
import functools
import math

import jax
import jax.numpy as jnp
from jax import lax
from jax.experimental import pallas as pl
from jax.experimental.pallas import tpu as pltpu
from jax.sharding import PartitionSpec as P

LANES = 128
STEP = 512
GRANT = 58 * 1024 * 1024
f32 = jnp.float32
bf16 = jnp.bfloat16


def band(base, index, span):
    row = jnp.broadcast_to(base[index : index + 1], (span, 2 * span))
    return pltpu.roll(row, 0, 1, stride=1, stride_axis=0).astype(bf16)


def banded(base, column, first, owner, span, group):
    total = jnp.zeros(owner.shape, f32)
    for g in range(LANES // group):
        value = jnp.dot(band(base, first + g, span), column, preferred_element_type=f32)
        total = jnp.where(owner == g, value, total)
    return total


def conv_kernel(span, group, turn_ref, base_ref, rim_ref, product_ref, query_ref, *refs):
    gated_ref, conv_ref = refs[-2:]
    owner = lax.broadcasted_iota(jnp.int32, (span, 2 * LANES), 1) % LANES // group
    for start in range(0, query_ref.shape[1], LANES):
        cut = slice(start, start + LANES)
        late = product_ref[:, cut]
        early = jnp.concatenate([rim_ref[:, cut], late[:span]], 0)
        column = jnp.concatenate([early, late], 1)
        total = banded(base_ref[...], column, start // group, owner, span, group)
        conv = jnp.concatenate([total[:, :LANES], total[:, LANES:]], 0)
        conv_ref[:, cut] = conv
        gated_ref[:, cut] = (query_ref[:, cut].astype(f32) * conv).astype(bf16)


def conv_call(turn, base, rim, product, query, after, span, group):
    tokens, width = query.shape
    lanes = min(width, STEP)

    def block(rows):
        return pl.BlockSpec((rows, lanes), lambda i, turn: (0, i))

    return pl.pallas_call(
        functools.partial(conv_kernel, span, group),
        grid_spec=pltpu.PrefetchScalarGridSpec(
            num_scalar_prefetch=1,
            grid=(width // lanes,),
            in_specs=[
                pl.BlockSpec((lanes // group, 2 * span), lambda i, turn: (i, 0)),
                block(span),
                block(tokens),
                block(tokens),
            ]
            + [pl.BlockSpec(memory_space=pl.ANY)] * len(after),
            out_specs=[
                pl.BlockSpec((tokens, lanes), lambda i, turn: (0, i ^ turn[0])),
                block(tokens),
            ],
        ),
        out_shape=[
            jax.ShapeDtypeStruct((tokens, width), bf16),
            jax.ShapeDtypeStruct((tokens, width), f32),
        ],
        cost_estimate=pl.CostEstimate(
            flops=4 * span * tokens * width * LANES // group,
            bytes_accessed=12 * tokens * width,
            transcendentals=0,
        ),
        name="conv",
    )(turn, base, rim, product, query, *after)


def gate_kernel(span, turn_ref, grad_ref, conv_ref, query_ref, query_grad_ref, grad_conv_ref, grad_rim_ref):
    grad = grad_ref[...].astype(f32)
    query_grad_ref[...] = (grad * conv_ref[...]).astype(bf16)
    grad_conv = (grad * query_ref[...].astype(f32)).astype(bf16)
    grad_conv_ref[...] = grad_conv
    grad_rim_ref[...] = grad_conv[:span]


def gate_call(turn, grad, conv, query, span):
    tokens, width = query.shape
    lanes = min(width, STEP)

    def block(rows):
        return pl.BlockSpec((rows, lanes), lambda i, turn: (0, i))

    return pl.pallas_call(
        functools.partial(gate_kernel, span),
        grid_spec=pltpu.PrefetchScalarGridSpec(
            num_scalar_prefetch=1,
            grid=(width // lanes,),
            in_specs=[
                pl.BlockSpec((tokens, lanes), lambda i, turn: (0, i ^ turn[0])),
                block(tokens),
                block(tokens),
            ],
            out_specs=[block(tokens), block(tokens), block(span)],
        ),
        out_shape=[
            jax.ShapeDtypeStruct((tokens, width), bf16),
            jax.ShapeDtypeStruct((tokens, width), bf16),
            jax.ShapeDtypeStruct((span, width), bf16),
        ],
        cost_estimate=pl.CostEstimate(flops=2 * tokens * width, bytes_accessed=12 * tokens * width, transcendentals=0),
        name="gate",
    )(turn, grad, conv, query)


def taps_kernel(span, group, grad_conv_ref, rim_ref, product_ref, *refs):
    taps_ref = refs[-1]
    rows = lax.broadcasted_iota(jnp.int32, (span, span), 0)
    columns = lax.broadcasted_iota(jnp.int32, (span, span), 1)
    flip = jnp.where(rows + columns == span - 1, 1.0, 0.0).astype(bf16)
    owner = lax.broadcasted_iota(jnp.int32, (span, 2 * LANES), 1) % LANES // group
    for start in range(0, grad_conv_ref.shape[1], LANES):
        cut = slice(start, start + LANES)
        grad_conv = grad_conv_ref[:, cut]
        left = jnp.concatenate([grad_conv[:span], grad_conv[span:]], 1)
        left = jnp.dot(flip, left, preferred_element_type=f32).astype(bf16)
        late = product_ref[:, cut]
        early = jnp.concatenate([rim_ref[:, cut], late[:span]], 0)
        right = jnp.concatenate([early, late], 1)
        for g in range(LANES // group):
            one = jnp.where(owner == g, left, jnp.zeros_like(left))
            corr = lax.dot_general(one, right, (((1,), (1,)), ((), ())), preferred_element_type=f32)
            lined = pltpu.roll(corr, 0, 1, stride=1, stride_axis=0)
            at = start // group + g
            taps_ref[at : at + 1] = jnp.sum(lined[:, span:], axis=0, keepdims=True)


def taps_call(grad_conv, rim, product, after, span, group):
    tokens, width = grad_conv.shape
    lanes = min(width, STEP)

    def block(rows):
        return pl.BlockSpec((rows, lanes), lambda i: (0, i))

    return pl.pallas_call(
        functools.partial(taps_kernel, span, group),
        grid=(width // lanes,),
        in_specs=[block(tokens), block(span), block(tokens)] + [pl.BlockSpec(memory_space=pl.ANY)] * len(after),
        out_specs=pl.BlockSpec((lanes // group, span), lambda i: (i, 0)),
        out_shape=jax.ShapeDtypeStruct((width // group, span), f32),
        cost_estimate=pl.CostEstimate(
            flops=8 * span * tokens * width * LANES // group,
            bytes_accessed=5 * tokens * width,
            transcendentals=0,
        ),
        name="taps",
    )(grad_conv, rim, product, *after)


def back_kernel(span, group, base_ref, grad_conv_ref, rim_ref, key_ref, value_ref, *refs):
    key_grad_ref, value_grad_ref = refs[-2:]
    owner = lax.broadcasted_iota(jnp.int32, (span, 2 * LANES), 1) % LANES // group
    for start in range(0, key_ref.shape[1], LANES):
        cut = slice(start, start + LANES)
        here = grad_conv_ref[:, cut]
        after = jnp.concatenate([here[span:], rim_ref[:, cut]], 0)
        column = jnp.concatenate([here, after], 1)
        total = banded(base_ref[...], column, start // group, owner, span, group)
        product = jnp.concatenate([total[:, :LANES], total[:, LANES:]], 0)
        key_grad_ref[:, cut] = (product * value_ref[:, cut].astype(f32)).astype(bf16)
        value_grad_ref[:, cut] = (product * key_ref[:, cut].astype(f32)).astype(bf16)


def back_call(base, grad_conv, rim, key, value, after, span, group):
    tokens, width = key.shape
    lanes = min(width, STEP)

    def block(rows):
        return pl.BlockSpec((rows, lanes), lambda i: (0, i))

    return pl.pallas_call(
        functools.partial(back_kernel, span, group),
        grid=(width // lanes,),
        in_specs=[
            pl.BlockSpec((lanes // group, 2 * span), lambda i: (i, 0)),
            block(tokens),
            block(span),
            block(tokens),
            block(tokens),
        ]
        + [pl.BlockSpec(memory_space=pl.ANY)] * len(after),
        out_specs=[block(tokens), block(tokens)],
        out_shape=[
            jax.ShapeDtypeStruct((tokens, width), bf16),
            jax.ShapeDtypeStruct((tokens, width), bf16),
        ],
        cost_estimate=pl.CostEstimate(
            flops=4 * span * tokens * width * LANES // group,
            bytes_accessed=12 * tokens * width,
            transcendentals=0,
        ),
        name="back",
    )(base, grad_conv, rim, key, value, *after)


def from_behind(shard, by):
    size = lax.axis_size("row")
    pairs = [(i, i + by) for i in range(size) if 0 <= i + by < size]
    return lax.ppermute(shard, "row", pairs)


def exchange(shard, bits):
    size = lax.axis_size("row")
    return lax.ppermute(shard, "row", [(i, i ^ bits) for i in range(size)])


def ring(shard):
    size = lax.axis_size("col")
    return lax.ppermute(shard, "col", [(i, (i + 1) % size) for i in range(size)])


def dot_nt(a, b):
    return lax.dot_general(a, b, (((1,), (1,)), ((), ())), preferred_element_type=f32)


def dot_tn(a, b):
    return lax.dot_general(a, b, (((0,), (0,)), ((), ())), preferred_element_type=f32)


def keep_kernel(*refs):
    pass


def once(array, *others):
    anywhere = pl.BlockSpec(memory_space=pl.ANY)
    return pl.pallas_call(
        keep_kernel,
        in_specs=[anywhere] * (1 + len(others)),
        out_specs=anywhere,
        out_shape=jax.ShapeDtypeStruct(array.shape, array.dtype),
        input_output_aliases={0: 0},
        name="once",
    )(array, *others)


def pick_kernel(at_ref, *refs):
    pieces, out_ref = refs[:4], refs[-1]
    for place, piece in enumerate(pieces):

        @pl.when(at_ref[0] == place)
        def _(piece=piece):
            pltpu.sync_copy(piece, out_ref)


def pick(pieces, at):
    return pl.pallas_call(
        pick_kernel,
        in_specs=[pl.BlockSpec(memory_space=pltpu.SMEM)] + [pl.BlockSpec(memory_space=pl.ANY)] * 4,
        out_specs=pl.BlockSpec(memory_space=pltpu.VMEM),
        out_shape=jax.ShapeDtypeStruct(pieces[0].shape, pieces[0].dtype),
        cost_estimate=pl.CostEstimate(flops=0, bytes_accessed=4 * pieces[0].size, transcendentals=0),
        name="pick",
    )(at.astype(jnp.int32).reshape(1), *pieces)


def copy_kernel(at_ref, in_ref, out_ref):
    out_ref[...] = in_ref[0]


def take(stack, at):
    _, rows, columns = stack.shape
    part = rows // 4
    return pl.pallas_call(
        copy_kernel,
        grid_spec=pltpu.PrefetchScalarGridSpec(
            num_scalar_prefetch=1,
            grid=(4,),
            in_specs=[pl.BlockSpec((1, part, columns), lambda i, at: (at[0], i, 0))],
            out_specs=pl.BlockSpec((part, columns), lambda i, at: (i, 0)),
        ),
        out_shape=jax.ShapeDtypeStruct((rows, columns), stack.dtype),
        cost_estimate=pl.CostEstimate(flops=0, bytes_accessed=4 * rows * columns, transcendentals=0),
        name="take",
    )(at.astype(jnp.int32).reshape(1), stack)


def add_kernel(parts, at_ref, *refs):
    pieces, came = refs[:4], refs[4]
    out_ref, held_ref, came_ref, sems = refs[-4:]
    rows = held_ref.shape[0] // parts

    def copies(source, target, which):
        for part in range(parts):
            cut = pl.ds(part * rows, rows)
            yield pltpu.make_async_copy(source.at[cut], target.at[cut], sems.at[which, part])

    for place, piece in enumerate(pieces):

        @pl.when(at_ref[0] == place)
        def _(piece=piece):
            pairs = list(zip(copies(piece, held_ref, 0), copies(came, came_ref, 1)))
            for one, other in pairs:
                one.start()
                other.start()
            for part, (one, other) in enumerate(pairs):
                one.wait()
                other.wait()
                cut = slice(part * rows, (part + 1) * rows)
                out_ref[cut] = (held_ref[cut].astype(f32) + came_ref[cut].astype(f32)).astype(bf16)


def pick_and_add(pieces, at, came, after):
    anywhere = pl.BlockSpec(memory_space=pl.ANY)
    parts = 4
    return pl.pallas_call(
        functools.partial(add_kernel, parts),
        in_specs=[pl.BlockSpec(memory_space=pltpu.SMEM)] + [anywhere] * (5 + len(after)),
        out_specs=pl.BlockSpec(memory_space=pltpu.VMEM),
        out_shape=jax.ShapeDtypeStruct(came.shape, bf16),
        scratch_shapes=[
            pltpu.VMEM(came.shape, bf16),
            pltpu.VMEM(came.shape, bf16),
            pltpu.SemaphoreType.DMA((2, parts)),
        ],
        cost_estimate=pl.CostEstimate(flops=came.size, bytes_accessed=6 * came.size, transcendentals=0),
        name="add",
    )(at.astype(jnp.int32).reshape(1), *pieces, came, *after)


def product_kernel(count, gradient, *refs):
    pieces, (own_ref, other_ref) = refs[:count], refs[count : count + 2]
    left_ref = refs[-1]
    step = pl.program_id(0)

    @pl.when(step == 0)
    def _():
        at = 0
        for piece in pieces:
            left_ref[at : at + piece.shape[0]] = piece[...]
            at += piece.shape[0]

    def write(value):
        at = 0
        for out in refs[-1 - gradient[1] : -1]:
            out[...] = value[at : at + out.shape[0]].astype(bf16)
            at += out.shape[0]

    if gradient[0]:
        steps = pl.num_programs(0) // 2

        @pl.when(step < steps)
        def _():
            write(dot_nt(left_ref[...], own_ref[...]))

        @pl.when(step >= steps)
        def _():
            write(dot_nt(left_ref[...], other_ref[...]))
    else:
        half = own_ref.shape[0]
        value = jnp.dot(left_ref[:, :half], own_ref[...], preferred_element_type=f32)
        value = value + jnp.dot(left_ref[:, half:], other_ref[...], preferred_element_type=f32)
        write(value)


def product_call(pieces, own, other, after, outs, gradient):
    block = 256
    rows = sum(piece.shape[0] for piece in pieces)
    depth = pieces[0].shape[1]
    if gradient:
        count = own.shape[0] // block
        columns = 2 * own.shape[0]
        specs = [
            pl.BlockSpec((block, depth), lambda i: (jnp.minimum(i, count - 1), 0)),
            pl.BlockSpec((block, depth), lambda i: (jnp.maximum(i - count, 0), 0)),
        ]
    else:
        columns = own.shape[1]
        specs = [pl.BlockSpec((own.shape[0], block), lambda i: (0, i))] * 2
    return list(
        pl.pallas_call(
            functools.partial(product_kernel, len(pieces), (gradient, outs)),
            grid=(columns // block,),
            in_specs=[pl.BlockSpec(piece.shape, lambda i: (0, 0)) for piece in pieces]
            + specs
            + [pl.BlockSpec(memory_space=pl.ANY)] * len(after),
            out_specs=[pl.BlockSpec((rows // outs, block), lambda i: (0, i))] * outs,
            out_shape=[jax.ShapeDtypeStruct((rows // outs, columns), bf16)] * outs,
            scratch_shapes=[pltpu.VMEM((rows, depth), bf16)],
            compiler_params=pltpu.CompilerParams(vmem_limit_bytes=GRANT),
            cost_estimate=pl.CostEstimate(
                flops=2 * rows * depth * columns,
                bytes_accessed=2 * (rows * depth + depth * columns + rows * columns),
                transcendentals=0,
            ),
            name="product",
        )(*pieces, own, other, *after)
    )


def weight_kernel(pieces, scale, *refs):
    held, grads, came = refs[:4], refs[4 : 4 + pieces], refs[4 + pieces : 8 + pieces]
    right_ref = refs[-1]
    step = pl.program_id(0)

    @pl.when(step == 0)
    def _():
        at = 0
        for piece in grads:
            right_ref[at : at + piece.shape[0]] = piece[...]
            at += piece.shape[0]

    left = jnp.concatenate([piece[...] for piece in held], 0)
    value = dot_tn(left, right_ref[...])
    if scale is None:
        for place, out_ref in enumerate(refs[-5:-1]):

            @pl.when(step == place)
            def _(out_ref=out_ref):
                out_ref[...] = value.astype(bf16)
    else:
        for place, came_ref in enumerate(came):

            @pl.when(step == place)
            def _(came_ref=came_ref):
                refs[-2][...] = ((value + came_ref[...].astype(f32)) * scale).astype(bf16)


def weight_call(held, grads, came, after, first, scale):
    width, columns = held[0].shape[1] // 2, grads[0].shape[1]
    block = width // 4
    tokens = held[0].shape[0]
    rows = tokens * len(held)
    return pl.pallas_call(
        functools.partial(weight_kernel, len(grads), scale),
        grid=(width // block,),
        in_specs=[pl.BlockSpec((tokens, block), lambda i: (0, first // block + i))] * len(held)
        + [pl.BlockSpec(piece.shape, lambda i: (0, 0)) for piece in grads]
        + [pl.BlockSpec((block, columns), lambda i: (0, 0))] * len(came)
        + [pl.BlockSpec(memory_space=pl.ANY)] * len(after),
        out_specs=pl.BlockSpec((block, columns), lambda i: (i, 0))
        if came
        else [pl.BlockSpec((block, columns), lambda i: (0, 0))] * 4,
        out_shape=jax.ShapeDtypeStruct((width, columns), bf16)
        if came
        else [jax.ShapeDtypeStruct((block, columns), bf16)] * 4,
        scratch_shapes=[pltpu.VMEM((rows, columns), bf16)],
        compiler_params=pltpu.CompilerParams(vmem_limit_bytes=GRANT),
        cost_estimate=pl.CostEstimate(
            flops=2 * rows * width * columns,
            bytes_accessed=2 * rows * (width + columns) + 4 * width * columns,
            transcendentals=0,
        ),
        name="weight",
    )(*held, *grads, *came, *after)


def projection(gated, out_weight, other_weight, out_grad, neighbours, total_tokens):
    chip = lax.axis_index("row") // 2
    plane = lax.axis_index("col")
    tokens = gated.shape[0]
    half, part = out_weight.shape[0], tokens // 2
    weights = (out_weight, other_weight)

    panel = lax.all_gather(gated, "col")
    kept = product_call([out_grad], *weights, [gated], 1, True)[0]
    grad_x, grad_y = [once(piece, kept) for piece in neighbours]
    far_x, far_y = grad_x[:part], grad_y[part:]
    far = [exchange(far_x, 4), exchange(far_y, 2)]
    grads = [out_grad, grad_x, grad_y, *far]

    to_x = product_call([grad_x], *weights, [far_x, far_y], 1, True)[0]
    to_y = product_call([grad_y], *weights, [to_x], 1, True)[0]
    to_far = product_call(far, *weights, [to_y], 1, True)[0]
    back_x, back_y = exchange(to_x, 2), exchange(to_y, 4)
    partial = [kept, back_x, back_y, exchange(to_far, 6)]

    def add(step, total, *after):
        return pick_and_add(partial, chip ^ (plane + 7 - step) % 4, ring(total), after)

    first = add(1, pick(partial, chip ^ (plane + 3) % 4))

    held = [take(panel, chip ^ d) for d in range(4)]
    held_x, held_y = exchange(held[1], 2), exchange(held[2], 4)
    held_far = exchange(once(held[3], held_x, held_y), 6)
    near = product_call([held_x, held_y], *weights, [first], 2, False)
    mixed_x, mixed_y = exchange(near[0], 2), exchange(near[1], 4)
    second = add(2, first, near[0])
    last = product_call([held[0], held_far], *weights, [near[0], second], 2, False)
    mixed_far = exchange(last[1], 6)
    held = [held[0], held_x, held_y, held_far]
    sent = weight_call(held, grads, [], [last[0], second], half, None)
    third = add(3, second, *sent[:1], mixed_x, mixed_y)
    mixed = (last[0].astype(f32) + mixed_x.astype(f32) + mixed_y.astype(f32) + mixed_far.astype(f32)).astype(bf16)

    came = [exchange(block, 1) for block in sent]

    def weight_half(after):
        return weight_call(held, grads, came, after, 0, 1.0 / math.sqrt(total_tokens))

    return mixed, third, weight_half


def projection_gathered(gated, out_weight, _, out_grad, neighbours, total_tokens):
    panel = lax.all_gather(gated, "col", axis=1, tiled=True)
    weights = lax.all_gather(out_weight, "row", axis=0, tiled=True)
    mixed = jnp.dot(panel, weights, preferred_element_type=f32).astype(bf16)
    partial = dot_nt(out_grad, weights).astype(bf16)
    grad_gated = lax.psum_scatter(partial, "col", scatter_dimension=1, tiled=True)
    weight_sum = lax.psum_scatter(
        dot_tn(panel, out_grad).astype(bf16), "row", scatter_dimension=0, tiled=True
    ).astype(f32)
    weight_grad = (weight_sum * (1.0 / math.sqrt(total_tokens))).astype(bf16)
    return mixed, grad_gated, lambda after: weight_grad


def shards(query_in, key_in, value_in, filters, out_weight, out_grad):
    tokens, width = query_in.shape
    groups, span = filters.shape
    group = width // groups
    rows, cols = lax.axis_size("row"), lax.axis_size("col")
    total_tokens = tokens * rows
    paired = rows == 2 * cols and cols == 4 and width == 2 * out_weight.shape[0] and width % (2 * STEP) == 0
    core = lax.axis_index("row") % 2
    turn = core * (width // STEP // 2) if paired else core * 0
    turn = turn.astype(jnp.int32).reshape(1)

    product = (key_in.astype(f32) * value_in.astype(f32)).astype(bf16)
    rim = from_behind(product[-span:], 1)
    zeros = jnp.zeros((groups, span - 1), f32)
    causal = jnp.concatenate([zeros[:, :1], filters[:, ::-1], zeros], 1)
    anticausal = jnp.concatenate([filters, zeros, zeros[:, :1]], 1)
    other_weight = exchange(out_weight, 1) if paired else product
    neighbours = []
    if paired:
        neighbours = [exchange(out_grad, 2), exchange(out_grad, 4)]
    gated, conv = conv_call(turn, causal, rim, product, query_in, [other_weight], span, group)

    project = projection if paired else projection_gathered
    mixed, grad_gated, weight_half = project(gated, out_weight, other_weight, out_grad, neighbours, total_tokens)

    query_grad, grad_conv, grad_rim = gate_call(turn, grad_gated, conv, query_in, span)
    grad_rim = from_behind(grad_rim, -1)
    taps = taps_call(grad_conv, rim, product, [], span, group)
    weight_grad = weight_half([taps])
    taps = taps + once(exchange(taps, 1), weight_grad)
    key_grad, value_grad = back_call(anticausal, grad_conv, grad_rim, key_in, value_in, [taps], span, group)
    taps = taps + once(exchange(taps, 2), key_grad)
    bits = 4
    while bits < rows:
        taps = taps + exchange(taps, bits)
        bits *= 2
    filter_grad = taps[:, ::-1] * (1.0 / math.sqrt(total_tokens * group))
    return (mixed, query_grad, key_grad, value_grad, weight_grad, filter_grad)


def solution(mesh):
    placed = (
        P("row", "col"),
        P("row", "col"),
        P("row", "col"),
        P("col", None),
        P("row", "col"),
        P("row", "col"),
    )
    return jax.shard_map(
        shards,
        mesh=mesh,
        in_specs=placed,
        out_specs=(
            P("row", "col"),
            P("row", "col"),
            P("row", "col"),
            P("row", "col"),
            P("row", "col"),
            P("col", None),
        ),
        check_vma=False,
    )
```

```python
import functools
import math

import jax
import jax.numpy as jnp
from jax import lax
from jax.experimental import pallas as pl
from jax.experimental.pallas import tpu as pltpu
from jax.sharding import PartitionSpec as P

LANES = 128
STEP = 512
GRANT = 58 * 1024 * 1024
f32 = jnp.float32
bf16 = jnp.bfloat16


def band(base, index, span):
    row = jnp.broadcast_to(base[index : index + 1], (span, 2 * span))
    return pltpu.roll(row, 0, 1, stride=1, stride_axis=0).astype(bf16)


def banded(base, column, first, owner, span, group):
    total = jnp.zeros(owner.shape, f32)
    for g in range(LANES // group):
        value = jnp.dot(band(base, first + g, span), column, preferred_element_type=f32)
        total = jnp.where(owner == g, value, total)
    return total


def conv_kernel(span, group, turn_ref, base_ref, rim_ref, product_ref, query_ref, *refs):
    gated_ref, conv_ref = refs[-2:]
    owner = lax.broadcasted_iota(jnp.int32, (span, 2 * LANES), 1) % LANES // group
    for start in range(0, query_ref.shape[1], LANES):
        cut = slice(start, start + LANES)
        late = product_ref[:, cut]
        early = jnp.concatenate([rim_ref[:, cut], late[:span]], 0)
        column = jnp.concatenate([early, late], 1)
        total = banded(base_ref[...], column, start // group, owner, span, group)
        conv = jnp.concatenate([total[:, :LANES], total[:, LANES:]], 0)
        conv_ref[:, cut] = conv
        gated_ref[:, cut] = (query_ref[:, cut].astype(f32) * conv).astype(bf16)


def conv_call(turn, base, rim, product, query, after, span, group):
    tokens, width = query.shape
    lanes = min(width, STEP)

    def block(rows):
        return pl.BlockSpec((rows, lanes), lambda i, turn: (0, i))

    return pl.pallas_call(
        functools.partial(conv_kernel, span, group),
        grid_spec=pltpu.PrefetchScalarGridSpec(
            num_scalar_prefetch=1,
            grid=(width // lanes,),
            in_specs=[
                pl.BlockSpec((lanes // group, 2 * span), lambda i, turn: (i, 0)),
                block(span),
                block(tokens),
                block(tokens),
            ]
            + [pl.BlockSpec(memory_space=pl.ANY)] * len(after),
            out_specs=[
                pl.BlockSpec((tokens, lanes), lambda i, turn: (0, i ^ turn[0])),
                block(tokens),
            ],
        ),
        out_shape=[
            jax.ShapeDtypeStruct((tokens, width), bf16),
            jax.ShapeDtypeStruct((tokens, width), f32),
        ],
        name="conv",
    )(turn, base, rim, product, query, *after)


def gate_kernel(span, turn_ref, grad_ref, conv_ref, query_ref, query_grad_ref, grad_conv_ref, grad_rim_ref):
    grad = grad_ref[...].astype(f32)
    query_grad_ref[...] = (grad * conv_ref[...]).astype(bf16)
    grad_conv = (grad * query_ref[...].astype(f32)).astype(bf16)
    grad_conv_ref[...] = grad_conv
    grad_rim_ref[...] = grad_conv[:span]


def gate_call(turn, grad, conv, query, span):
    tokens, width = query.shape
    lanes = min(width, STEP)

    def block(rows):
        return pl.BlockSpec((rows, lanes), lambda i, turn: (0, i))

    return pl.pallas_call(
        functools.partial(gate_kernel, span),
        grid_spec=pltpu.PrefetchScalarGridSpec(
            num_scalar_prefetch=1,
            grid=(width // lanes,),
            in_specs=[
                pl.BlockSpec((tokens, lanes), lambda i, turn: (0, i ^ turn[0])),
                block(tokens),
                block(tokens),
            ],
            out_specs=[block(tokens), block(tokens), block(span)],
        ),
        out_shape=[
            jax.ShapeDtypeStruct((tokens, width), bf16),
            jax.ShapeDtypeStruct((tokens, width), bf16),
            jax.ShapeDtypeStruct((span, width), bf16),
        ],
        name="gate",
    )(turn, grad, conv, query)


def taps_kernel(span, group, grad_conv_ref, rim_ref, product_ref, *refs):
    taps_ref = refs[-1]
    rows = lax.broadcasted_iota(jnp.int32, (span, span), 0)
    columns = lax.broadcasted_iota(jnp.int32, (span, span), 1)
    flip = jnp.where(rows + columns == span - 1, 1.0, 0.0).astype(bf16)
    owner = lax.broadcasted_iota(jnp.int32, (span, 2 * LANES), 1) % LANES // group
    for start in range(0, grad_conv_ref.shape[1], LANES):
        cut = slice(start, start + LANES)
        grad_conv = grad_conv_ref[:, cut]
        left = jnp.concatenate([grad_conv[:span], grad_conv[span:]], 1)
        left = jnp.dot(flip, left, preferred_element_type=f32).astype(bf16)
        late = product_ref[:, cut]
        early = jnp.concatenate([rim_ref[:, cut], late[:span]], 0)
        right = jnp.concatenate([early, late], 1)
        for g in range(LANES // group):
            one = jnp.where(owner == g, left, jnp.zeros_like(left))
            corr = lax.dot_general(one, right, (((1,), (1,)), ((), ())), preferred_element_type=f32)
            lined = pltpu.roll(corr, 0, 1, stride=1, stride_axis=0)
            at = start // group + g
            taps_ref[at : at + 1] = jnp.sum(lined[:, span:], axis=0, keepdims=True)


def taps_call(grad_conv, rim, product, after, span, group):
    tokens, width = grad_conv.shape
    lanes = min(width, STEP)

    def block(rows):
        return pl.BlockSpec((rows, lanes), lambda i: (0, i))

    return pl.pallas_call(
        functools.partial(taps_kernel, span, group),
        grid=(width // lanes,),
        in_specs=[block(tokens), block(span), block(tokens)] + [pl.BlockSpec(memory_space=pl.ANY)] * len(after),
        out_specs=pl.BlockSpec((lanes // group, span), lambda i: (i, 0)),
        out_shape=jax.ShapeDtypeStruct((width // group, span), f32),
        name="taps",
    )(grad_conv, rim, product, *after)


def back_kernel(span, group, base_ref, grad_conv_ref, rim_ref, key_ref, value_ref, *refs):
    key_grad_ref, value_grad_ref = refs[-2:]
    owner = lax.broadcasted_iota(jnp.int32, (span, 2 * LANES), 1) % LANES // group
    for start in range(0, key_ref.shape[1], LANES):
        cut = slice(start, start + LANES)
        here = grad_conv_ref[:, cut]
        after = jnp.concatenate([here[span:], rim_ref[:, cut]], 0)
        column = jnp.concatenate([here, after], 1)
        total = banded(base_ref[...], column, start // group, owner, span, group)
        product = jnp.concatenate([total[:, :LANES], total[:, LANES:]], 0)
        key_grad_ref[:, cut] = (product * value_ref[:, cut].astype(f32)).astype(bf16)
        value_grad_ref[:, cut] = (product * key_ref[:, cut].astype(f32)).astype(bf16)


def back_call(base, grad_conv, rim, key, value, after, span, group):
    tokens, width = key.shape
    lanes = min(width, STEP)

    def block(rows):
        return pl.BlockSpec((rows, lanes), lambda i: (0, i))

    return pl.pallas_call(
        functools.partial(back_kernel, span, group),
        grid=(width // lanes,),
        in_specs=[
            pl.BlockSpec((lanes // group, 2 * span), lambda i: (i, 0)),
            block(tokens),
            block(span),
            block(tokens),
            block(tokens),
        ]
        + [pl.BlockSpec(memory_space=pl.ANY)] * len(after),
        out_specs=[block(tokens), block(tokens)],
        out_shape=[
            jax.ShapeDtypeStruct((tokens, width), bf16),
            jax.ShapeDtypeStruct((tokens, width), bf16),
        ],
        name="back",
    )(base, grad_conv, rim, key, value, *after)


def from_behind(shard, by):
    size = lax.axis_size("row")
    pairs = [(i, i + by) for i in range(size) if 0 <= i + by < size]
    return lax.ppermute(shard, "row", pairs)


def exchange(shard, bits):
    size = lax.axis_size("row")
    return lax.ppermute(shard, "row", [(i, i ^ bits) for i in range(size)])


def ring(shard):
    size = lax.axis_size("col")
    return lax.ppermute(shard, "col", [(i, (i + 1) % size) for i in range(size)])


def dot_nt(a, b):
    return lax.dot_general(a, b, (((1,), (1,)), ((), ())), preferred_element_type=f32)


def dot_tn(a, b):
    return lax.dot_general(a, b, (((0,), (0,)), ((), ())), preferred_element_type=f32)


def keep_kernel(*refs):
    pass


def once(array, *others):
    anywhere = pl.BlockSpec(memory_space=pl.ANY)
    return pl.pallas_call(
        keep_kernel,
        in_specs=[anywhere] * (1 + len(others)),
        out_specs=anywhere,
        out_shape=jax.ShapeDtypeStruct(array.shape, array.dtype),
        input_output_aliases={0: 0},
        name="once",
    )(array, *others)


def pick_kernel(at_ref, *refs):
    pieces, out_ref = refs[:4], refs[-1]
    for place, piece in enumerate(pieces):

        @pl.when(at_ref[0] == place)
        def _(piece=piece):
            pltpu.sync_copy(piece, out_ref)


def pick(pieces, at):
    return pl.pallas_call(
        pick_kernel,
        in_specs=[pl.BlockSpec(memory_space=pltpu.SMEM)] + [pl.BlockSpec(memory_space=pl.ANY)] * 4,
        out_specs=pl.BlockSpec(memory_space=pltpu.VMEM),
        out_shape=jax.ShapeDtypeStruct(pieces[0].shape, pieces[0].dtype),
        name="pick",
    )(at.astype(jnp.int32).reshape(1), *pieces)


def add_kernel(parts, at_ref, *refs):
    pieces, came = refs[:4], refs[4]
    out_ref, held_ref, came_ref, sems = refs[-4:]
    rows = held_ref.shape[0] // parts

    def copies(source, target, which):
        for part in range(parts):
            cut = pl.ds(part * rows, rows)
            yield pltpu.make_async_copy(source.at[cut], target.at[cut], sems.at[which, part])

    for place, piece in enumerate(pieces):

        @pl.when(at_ref[0] == place)
        def _(piece=piece):
            pairs = list(zip(copies(piece, held_ref, 0), copies(came, came_ref, 1)))
            for one, other in pairs:
                one.start()
                other.start()
            for part, (one, other) in enumerate(pairs):
                one.wait()
                other.wait()
                cut = slice(part * rows, (part + 1) * rows)
                out_ref[cut] = (held_ref[cut].astype(f32) + came_ref[cut].astype(f32)).astype(bf16)


def pick_and_add(pieces, at, came, after):
    anywhere = pl.BlockSpec(memory_space=pl.ANY)
    parts = 4
    return pl.pallas_call(
        functools.partial(add_kernel, parts),
        in_specs=[pl.BlockSpec(memory_space=pltpu.SMEM)] + [anywhere] * (5 + len(after)),
        out_specs=pl.BlockSpec(memory_space=pltpu.VMEM),
        out_shape=jax.ShapeDtypeStruct(came.shape, bf16),
        scratch_shapes=[
            pltpu.VMEM(came.shape, bf16),
            pltpu.VMEM(came.shape, bf16),
            pltpu.SemaphoreType.DMA((2, parts)),
        ],
        name="add",
    )(at.astype(jnp.int32).reshape(1), *pieces, came, *after)


def product_kernel(count, gradient, *refs):
    pieces, (own_ref, other_ref) = refs[:count], refs[count : count + 2]
    left_ref = refs[-1]
    step = pl.program_id(0)

    @pl.when(step == 0)
    def _():
        at = 0
        for piece in pieces:
            left_ref[at : at + piece.shape[0]] = piece[...]
            at += piece.shape[0]

    def write(value):
        at = 0
        for out in refs[-1 - gradient[1] : -1]:
            out[...] = value[at : at + out.shape[0]].astype(bf16)
            at += out.shape[0]

    if gradient[0]:
        steps = pl.num_programs(0) // 2

        @pl.when(step < steps)
        def _():
            write(dot_nt(left_ref[...], own_ref[...]))

        @pl.when(step >= steps)
        def _():
            write(dot_nt(left_ref[...], other_ref[...]))
    else:
        half = own_ref.shape[0]
        value = jnp.dot(left_ref[:, :half], own_ref[...], preferred_element_type=f32)
        value = value + jnp.dot(left_ref[:, half:], other_ref[...], preferred_element_type=f32)
        write(value)


def product_call(pieces, own, other, after, outs, gradient):
    block = 512
    rows = sum(piece.shape[0] for piece in pieces)
    depth = pieces[0].shape[1]
    if gradient:
        count = own.shape[0] // block
        columns = 2 * own.shape[0]
        specs = [
            pl.BlockSpec((block, depth), lambda i: (jnp.minimum(i, count - 1), 0)),
            pl.BlockSpec((block, depth), lambda i: (jnp.maximum(i - count, 0), 0)),
        ]
    else:
        columns = own.shape[1]
        specs = [pl.BlockSpec((own.shape[0], block), lambda i: (0, i))] * 2
    return list(
        pl.pallas_call(
            functools.partial(product_kernel, len(pieces), (gradient, outs)),
            grid=(columns // block,),
            in_specs=[pl.BlockSpec(piece.shape, lambda i: (0, 0)) for piece in pieces]
            + specs
            + [pl.BlockSpec(memory_space=pl.ANY)] * len(after),
            out_specs=[pl.BlockSpec((rows // outs, block), lambda i: (0, i))] * outs,
            out_shape=[jax.ShapeDtypeStruct((rows // outs, columns), bf16)] * outs,
            scratch_shapes=[pltpu.VMEM((rows, depth), bf16)],
            compiler_params=pltpu.CompilerParams(vmem_limit_bytes=GRANT),
            name="product",
        )(*pieces, own, other, *after)
    )


def weight_kernel(pieces, scale, *refs):
    held, grads, came = refs[:4], refs[4 : 4 + pieces], refs[4 + pieces : 8 + pieces]
    right_ref = refs[-1]
    step = pl.program_id(0)

    @pl.when(step == 0)
    def _():
        at = 0
        for piece in grads:
            right_ref[at : at + piece.shape[0]] = piece[...]
            at += piece.shape[0]

    left = jnp.concatenate([piece[...] for piece in held], 0)
    value = dot_tn(left, right_ref[...])
    if scale is None:
        for place, out_ref in enumerate(refs[-5:-1]):

            @pl.when(step == place)
            def _(out_ref=out_ref):
                out_ref[...] = value.astype(bf16)
    else:
        for place, came_ref in enumerate(came):

            @pl.when(step == place)
            def _(came_ref=came_ref):
                refs[-2][...] = ((value + came_ref[...].astype(f32)) * scale).astype(bf16)


def weight_call(held, grads, came, after, first, scale):
    width, columns = held[0].shape[1] // 2, grads[0].shape[1]
    block = width // 4
    tokens = held[0].shape[0]
    rows = tokens * len(held)
    return pl.pallas_call(
        functools.partial(weight_kernel, len(grads), scale),
        grid=(width // block,),
        in_specs=[pl.BlockSpec((tokens, block), lambda i: (0, first // block + i))] * len(held)
        + [pl.BlockSpec(piece.shape, lambda i: (0, 0)) for piece in grads]
        + [pl.BlockSpec((block, columns), lambda i: (0, 0))] * len(came)
        + [pl.BlockSpec(memory_space=pl.ANY)] * len(after),
        out_specs=pl.BlockSpec((block, columns), lambda i: (i, 0))
        if came
        else [pl.BlockSpec((block, columns), lambda i: (0, 0))] * 4,
        out_shape=jax.ShapeDtypeStruct((width, columns), bf16)
        if came
        else [jax.ShapeDtypeStruct((block, columns), bf16)] * 4,
        scratch_shapes=[pltpu.VMEM((rows, columns), bf16)],
        compiler_params=pltpu.CompilerParams(vmem_limit_bytes=GRANT),
        name="weight",
    )(*held, *grads, *came, *after)


def projection(gated, out_weight, other_weight, out_grad, neighbours, total_tokens):
    chip = lax.axis_index("row") // 2
    plane = lax.axis_index("col")
    tokens = gated.shape[0]
    half, part = out_weight.shape[0], tokens // 2
    weights = (out_weight, other_weight)

    kept = product_call([out_grad], *weights, [gated], 1, True)[0]
    grad_x, grad_y = [once(piece, kept) for piece in neighbours]
    far_x, far_y = grad_x[:part], grad_y[part:]
    far = [exchange(far_x, 4), exchange(far_y, 2)]
    grads = [out_grad, grad_x, grad_y, *far]

    to_x = product_call([grad_x], *weights, [far_x, far_y], 1, True)[0]
    z1 = once(ring(gated), to_x)
    z2 = ring(z1)
    to_y = product_call([grad_y], *weights, [z1], 1, True)[0]
    to_far = product_call(far, *weights, [to_y], 1, True)[0]
    z2 = once(z2, to_far)
    z3 = ring(z2)
    partial = [kept, exchange(to_x, 2), exchange(to_y, 4), exchange(to_far, 6)]

    def add(step, total, *after):
        return pick_and_add(partial, chip ^ (plane + 7 - step) % 4, ring(total), after)

    first = add(1, pick(partial, chip ^ (plane + 3) % 4))

    pieces = [gated, z1, z2, z3]
    held = [pick(pieces, (plane + 4 - (chip ^ d)) % 4) for d in range(4)]
    held_x, held_y = exchange(held[1], 2), exchange(held[2], 4)
    held_far = exchange(once(held[3], held_x, held_y), 6)
    near = product_call([held_x, held_y], *weights, [first], 2, False)
    mixed_x, mixed_y = exchange(near[0], 2), exchange(near[1], 4)
    second = add(2, first, near[0])
    last = product_call([held[0], held_far], *weights, [near[0], second], 2, False)
    mixed_far = exchange(last[1], 6)
    held = [held[0], held_x, held_y, held_far]
    sent = weight_call(held, grads, [], [last[0], second], half, None)
    third = add(3, second, *sent[:1], mixed_x, mixed_y)
    mixed = (last[0].astype(f32) + mixed_x.astype(f32) + mixed_y.astype(f32) + mixed_far.astype(f32)).astype(bf16)

    came = [exchange(block, 1) for block in sent]

    def weight_half(after):
        return weight_call(held, grads, came, after, 0, 1.0 / math.sqrt(total_tokens))

    return mixed, third, weight_half


def projection_gathered(gated, out_weight, _, out_grad, neighbours, total_tokens):
    panel = lax.all_gather(gated, "col", axis=1, tiled=True)
    weights = lax.all_gather(out_weight, "row", axis=0, tiled=True)
    mixed = jnp.dot(panel, weights, preferred_element_type=f32).astype(bf16)
    partial = dot_nt(out_grad, weights).astype(bf16)
    grad_gated = lax.psum_scatter(partial, "col", scatter_dimension=1, tiled=True)
    weight_sum = lax.psum_scatter(
        dot_tn(panel, out_grad).astype(bf16), "row", scatter_dimension=0, tiled=True
    ).astype(f32)
    weight_grad = (weight_sum * (1.0 / math.sqrt(total_tokens))).astype(bf16)
    return mixed, grad_gated, lambda after: weight_grad


def shards(query_in, key_in, value_in, filters, out_weight, out_grad):
    tokens, width = query_in.shape
    groups, span = filters.shape
    group = width // groups
    rows, cols = lax.axis_size("row"), lax.axis_size("col")
    total_tokens = tokens * rows
    paired = rows == 2 * cols and cols == 4 and width == 2 * out_weight.shape[0] and width % (2 * STEP) == 0
    core = lax.axis_index("row") % 2
    turn = core * (width // STEP // 2) if paired else core * 0
    turn = turn.astype(jnp.int32).reshape(1)

    product = (key_in.astype(f32) * value_in.astype(f32)).astype(bf16)
    rim = from_behind(product[-span:], 1)
    zeros = jnp.zeros((groups, span - 1), f32)
    causal = jnp.concatenate([zeros[:, :1], filters[:, ::-1], zeros], 1)
    anticausal = jnp.concatenate([filters, zeros, zeros[:, :1]], 1)
    other_weight = exchange(out_weight, 1) if paired else product
    neighbours = []
    if paired:
        neighbours = [exchange(out_grad, 2), exchange(out_grad, 4)]
    gated, conv = conv_call(turn, causal, rim, product, query_in, [other_weight], span, group)

    project = projection if paired else projection_gathered
    mixed, grad_gated, weight_half = project(gated, out_weight, other_weight, out_grad, neighbours, total_tokens)

    query_grad, grad_conv, grad_rim = gate_call(turn, grad_gated, conv, query_in, span)
    grad_rim = from_behind(grad_rim, -1)
    taps = taps_call(grad_conv, rim, product, [], span, group)
    weight_grad = weight_half([taps])
    taps = taps + once(exchange(taps, 1), weight_grad)
    key_grad, value_grad = back_call(anticausal, grad_conv, grad_rim, key_in, value_in, [taps], span, group)
    taps = taps + once(exchange(taps, 2), key_grad)
    bits = 4
    while bits < rows:
        taps = taps + exchange(taps, bits)
        bits *= 2
    filter_grad = taps[:, ::-1] * (1.0 / math.sqrt(total_tokens * group))
    return (mixed, query_grad, key_grad, value_grad, weight_grad, filter_grad)


def solution(mesh):
    placed = (
        P("row", "col"),
        P("row", "col"),
        P("row", "col"),
        P("col", None),
        P("row", "col"),
        P("row", "col"),
    )
    return jax.shard_map(
        shards,
        mesh=mesh,
        in_specs=placed,
        out_specs=(
            P("row", "col"),
            P("row", "col"),
            P("row", "col"),
            P("row", "col"),
            P("row", "col"),
            P("col", None),
        ),
        check_vma=False,
    )
```
